512 devices in a mesh: dp: 2 (over z_lo), gx: 8 (over y), gy: 4 (over x), gz: 8 (over z_hi, core).
Axes of the slice: x: 4, y: 8, z: 8 (z_hi: 4, z_lo: 2; z = z_hi * 2 + z_lo), core: 2. Of those that a mesh axis runs over, the one named last changes fastest.
Arguments:
- tokens: bfloat16 [1024, 4096], P(('dp', 'gx', 'gy'), 'gz'), may hold values from -6 to 6
- gate_weight: bfloat16 [4096, 14848], P('gz', ('gx', 'gy')), may hold values from -0.09375 to 0.09375
- up_weight: bfloat16 [4096, 14848], P('gz', ('gx', 'gy')), may hold values from -0.09375 to 0.09375
- down_weight: bfloat16 [14848, 4096], P(('gx', 'gy'), 'gz'), may hold values from -0.046875 to 0.046875
- out_grad: bfloat16 [1024, 4096], P(('dp', 'gx', 'gy'), 'gz'), may hold values from -6 to 6
Outputs:
- output: bfloat16 [1024, 4096], P(('dp', 'gx', 'gy'), 'gz')
- input_grad: bfloat16 [1024, 4096], P(('dp', 'gx', 'gy'), 'gz')
- gate_grad: bfloat16 [4096, 14848], P('gz', ('gx', 'gy'))
- up_grad: bfloat16 [4096, 14848], P('gz', ('gx', 'gy'))
- down_grad: bfloat16 [14848, 4096], P(('gx', 'gy'), 'gz')
The draws below stay inside these ranges and needn't reach their ends.
All inputs are finite; a program needn't handle non-finite values.
Results may differ from the reference program's by a relative error of at most 0.03.
Values may be sent and summed in bfloat16 or wider, within the bound.
A program may use at most 64 MiB of HBM per device.

```python
import jax
import jax.numpy as jnp
from jax import lax

D = 4096
F = 14848
TOKENS = 1024
N_GX = 8
N_GZ = 8


def block_levels(stream_key, shape, pieces, smallest, top_value):
    factor_of, own = 1.0, jax.random.fold_in(stream_key, 6)
    for position, parts in pieces:
        draws = jnp.exp(jax.random.uniform(jax.random.fold_in(own, position), (parts,), jnp.float32, smallest / len(pieces), top_value / len(pieces)))
        factor_of = factor_of * jnp.repeat(draws, shape[position] // parts).reshape([-1 if axis == position else 1 for axis in range(len(shape))])
    return factor_of


def bell_draw(stream_key, shape, deviation, most, cuts=(), held_as=jnp.bfloat16):
    result = deviation * jax.random.normal(stream_key, shape, jnp.float32)
    if cuts:
        result = result * block_levels(stream_key, shape, cuts, -0.22, 0.18)
    return jnp.clip(result, -most, most).astype(held_as)


def setup_inputs(seed: int = 0) -> dict:
    splits = jax.random.split(jax.random.key(seed), 6)
    return {
        "tokens": bell_draw(splits[0], (TOKENS, D), 1.0, 6.0, ((0, 64), (1, 8))),
        "gate_weight": bell_draw(splits[1], (D, F), D ** -0.5, 0.09375, ((0, 8), (1, 32))),
        "up_weight": bell_draw(splits[2], (D, F), D ** -0.5, 0.09375, ((0, 8), (1, 32))),
        "down_weight": bell_draw(splits[3], (F, D), F ** -0.5, 0.046875, ((0, 32), (1, 8))),
        "out_grad": bell_draw(splits[4], (TOKENS, D), 1.0, 6.0, ((0, 64), (1, 8))),
    }


def blocked_product(left, right, left_dim, right_dim, count):
    width = left.shape[left_dim] // count
    dims = (((left_dim,), (right_dim,)), ((), ()))
    out_rows = left.shape[1 - left_dim]
    out_cols = right.shape[1 - right_dim]

    def one_block(index, total):
        start = (index * width)
        start = jnp.asarray(start).astype(jnp.int32)
        part_left = lax.dynamic_slice_in_dim(left, start, width, left_dim)
        part_right = lax.dynamic_slice_in_dim(right, start, width, right_dim)
        term = lax.dot_general(part_left, part_right, dims, preferred_element_type=jnp.float32)
        return total + term.astype(jnp.bfloat16).astype(jnp.float32)

    return lax.fori_loop(0, count, one_block, jnp.zeros((out_rows, out_cols), jnp.float32))


def reference(tokens, gate_weight, up_weight, down_weight, out_grad):
    gate_val = blocked_product(tokens, gate_weight, 1, 0, N_GZ)
    up_val = blocked_product(tokens, up_weight, 1, 0, N_GZ)
    gate_sig = jax.nn.sigmoid(gate_val)
    gate_act = gate_val * gate_sig
    hidden = (gate_act * up_val).astype(jnp.bfloat16)
    output = blocked_product(hidden, down_weight, 1, 0, N_GX).astype(jnp.bfloat16)
    hid_grad = blocked_product(out_grad, down_weight, 1, 1, N_GZ)
    gate_delta = (hid_grad * up_val * gate_sig * (1.0 + gate_val * (1.0 - gate_sig))).astype(jnp.bfloat16)
    up_delta = (hid_grad * gate_act).astype(jnp.bfloat16)
    back_dims = (((1,), (1,)), ((), ()))
    input_grad = lax.dot_general(gate_delta, gate_weight, back_dims, preferred_element_type=jnp.float32)
    input_grad = input_grad + lax.dot_general(up_delta, up_weight, back_dims, preferred_element_type=jnp.float32)
    row_dims = (((0,), (0,)), ((), ()))
    gate_grad = lax.dot_general(tokens, gate_delta, row_dims, preferred_element_type=jnp.float32)
    up_grad = lax.dot_general(tokens, up_delta, row_dims, preferred_element_type=jnp.float32)
    down_grad = lax.dot_general(hidden, out_grad, row_dims, preferred_element_type=jnp.float32)
    return (output, input_grad.astype(jnp.bfloat16), gate_grad.astype(jnp.bfloat16),
            up_grad.astype(jnp.bfloat16), down_grad.astype(jnp.bfloat16))
```

```python
import jax
import jax.numpy as jnp
from jax import lax
from jax.experimental import pallas as pl
from jax.experimental.pallas import tpu as pltpu
from jax.sharding import PartitionSpec as P

BF = jnp.bfloat16
F32 = jnp.float32
HALF = 240
LAST = 224
NT = (((1,), (1,)), ((), ()))
TN = (((0,), (0,)), ((), ()))
NN = (((1,), (0,)), ((), ()))
FAR = (4, 3, 5, 2, 6, 1, 7)


def kernel(
    tok_ref, grad_ref, wg_ref, wu_ref, wd_ref,
    out_ref, ing_ref, gg_ref, ug_ref, dg_ref,
    T, W, PM, SC, RC, SZ, RZ, V, D, OB, RX, SY, RY, WG, FO,
    lsem, ssem, rsem,
):
    dp, gx, gy, gz = (lax.axis_index(a) for a in ("dp", "gx", "gy", "gz"))
    zh, c = lax.div(gz, 2), lax.rem(gz, 2)
    other = 1 - c
    odp = 1 - dp

    def ydev(k):
        return (dp, lax.rem(gx + k, 8), gy, gz)

    def xdev(k):
        return (dp, gx, lax.rem(gy + k, 4), gz)

    def zdev(k):
        return (dp, gx, gy, lax.rem(zh + k, 4) * 2 + c)

    core = (dp, gx, gy, zh * 2 + other)
    near_a = (odp, gx, gy, gz)
    near_b = (odp, gx, gy, lax.rem(zh + 3 + 2 * dp, 4) * 2 + c)

    count = [0]
    sent = []

    def send(src, dst, device):
        i = count[0]
        count[0] += 1
        copy = pltpu.make_async_remote_copy(
            src_ref=src,
            dst_ref=dst,
            send_sem=ssem.at[i],
            recv_sem=rsem.at[i],
            device_id=device,
            device_id_type=pl.DeviceIdType.MESH,
        )
        copy.start()
        sent.append(copy)
        return copy

    def arrive(copies):
        for copy in copies:
            copy.wait_recv()

    lcount = [0]

    def local(src, dst):
        i = lcount[0]
        lcount[0] += 1
        copy = pltpu.make_async_copy(src, dst, lsem.at[i])
        copy.start()
        return copy

    tok_in = [local(tok_ref, T.at[0, dp, gx, gy]), local(grad_ref, T.at[1, dp, gx, gy])]
    w_in = []
    for q, ref in enumerate((wg_ref, wu_ref, wd_ref)):
        w_in.append(local(ref.at[pl.ds(0, HALF)], W.at[q, 0]))
        w_in.append(local(ref.at[pl.ds(HALF, LAST)], W.at[q, 1, pl.ds(0, LAST)]))

    barrier = pltpu.get_barrier_semaphore()
    partners = [ydev(k) for k in FAR] + [xdev(k) for k in (2, 1, 3)] + [zdev(k) for k in (2, 1, 3)]
    partners += [near_a, near_b, core]
    for device in partners:
        pl.semaphore_signal(barrier, inc=1, device_id=device, device_id_type=pl.DeviceIdType.MESH)
    for q in range(3):
        W[q, 1, LAST:, :] = jnp.zeros((HALF - LAST, 512), BF)
    for copy in tok_in:
        copy.wait()
    pl.semaphore_wait(barrier, len(partners))

    def ysends(a, d, whole):
        ref = T.at[a, d, gx] if whole else T.at[a, d, gx, gy]
        return [send(ref, ref, ydev(k)) for k in FAR]

    def xsends(a, d, whole):
        ref = T.at[a, d, :, gy] if whole else T.at[a, d, gx, gy]
        return [send(ref, ref, xdev(k)) for k in (2, 1, 3)]

    tok_y = ysends(0, dp, False)
    grad_x = xsends(1, dp, False)
    swap = [send(T.at[a, dp, gx, gy], T.at[a, dp, gx, gy], near_a) for a in range(2)]
    arrive(tok_y)
    tok_x = xsends(0, dp, True)
    arrive(grad_x)
    grad_y = ysends(1, dp, True)
    for copy in w_in:
        copy.wait()
    arrive(tok_x)

    def project(q, x):
        far = lax.dot_general(W[q, other], x, NT, preferred_element_type=F32)
        for j in range(4):
            SC[q, j] = far[:, 128 * j : 128 * j + 128].astype(BF)
        copy = send(SC.at[q], RC.at[q], core)
        mine = lax.dot_general(W[q, c], x, NT, preferred_element_type=F32)
        for j in range(4):
            PM[q, j] = mine[:, 128 * j : 128 * j + 128]
        return copy

    def scatter(q, copy):
        copy.wait_recv()
        copies = []
        for k in (2, 1, 3):
            j = lax.rem(zh + k, 4)
            SZ[q, k - 1] = (PM[q, j] + RC[q, j].astype(F32)).astype(BF)
            copies.append(send(SZ.at[q, k - 1], RZ.at[q, k - 1], zdev(k)))
        return copies

    def total(q, copies):
        arrive(copies)
        value = PM[q, zh] + RC[q, zh].astype(F32)
        for k in range(3):
            value = value + RZ[q, k].astype(F32)
        return value

    x = T[0, dp].reshape(512, 512)
    gate_c = project(0, x)
    up_c = project(1, x)
    gate_z = scatter(0, gate_c)
    up_z = scatter(1, up_c)
    arrive(swap)
    other_y = ysends(0, odp, False)
    other_x = xsends(1, odp, False)
    arrive(grad_y)
    hg_c = project(2, T[1, dp].reshape(512, 512))
    hg_z = scatter(2, hg_c)
    arrive(other_y)
    other_y = xsends(0, odp, True)
    arrive(other_x)
    other_x = ysends(1, odp, True)

    def spread(q, value):
        D[q, dp, c, zh] = value.astype(BF)
        ref = D.at[q, dp, c, zh]
        return [send(ref, ref, zdev(k)) for k in (2, 1, 3)], [send(ref, ref, core)]

    gate_val = total(0, gate_z)
    up_val = total(1, up_z)
    gate_sig = jax.nn.sigmoid(gate_val)
    gate_act = gate_val * gate_sig
    V[0] = up_val * gate_sig * (1.0 + gate_val * (1.0 - gate_sig))
    V[1] = gate_act
    h_z, h_c = spread(0, gate_act * up_val)
    hid_grad = total(2, hg_z)
    gd_z, gd_c = spread(1, hid_grad * V[0])
    ud_z, ud_c = spread(2, hid_grad * V[1])

    def forward(q, copies, to_core):
        for k, copy in zip((2, 1, 3), copies, strict=True):
            copy.wait_recv()
            ref = D.at[q, dp, c, lax.rem(zh + 4 - k, 4)]
            to_core.append(send(ref, ref, core))

    def swap_dp(q):
        low, high = D.at[q, dp, c, pl.ds(0, 2)], D.at[q, dp, c, pl.ds(2, 2)]
        return [send(low, low, near_a), send(high, high, near_b)]

    def rows(q, d):
        halves = [
            jnp.concatenate([D[q, d, h, j] for j in range(4)], axis=1) for h in range(2)
        ]
        return jnp.concatenate(halves, axis=0)

    def x_scatter(o, part):
        OB[o] = part.astype(BF).reshape(8, 4, 16, 512)
        return [
            send(OB.at[o, :, lax.rem(gy + k, 4)], RX.at[o, k - 1], xdev(k)) for k in (2, 1, 3)
        ]

    def y_scatter(o, copies):
        arrive(copies)
        value = OB[o, :, gy].astype(F32)
        for k in range(3):
            value = value + RX[o, k].astype(F32)
        SY[o] = value.astype(BF)
        return [send(SY.at[o, lax.rem(gx + k, 8)], RY.at[o, k - 1], ydev(k)) for k in FAR]

    def finish(o, copies, ref):
        arrive(copies)
        value = SY[o, gx].astype(F32)
        for k in range(7):
            value = value + RY[o, k].astype(F32)
        FO[o] = value.astype(BF)
        return local(FO.at[o], ref)

    forward(0, h_z, h_c)
    arrive(h_c)
    out_x = x_scatter(0, lax.dot_general(rows(0, dp), W[2].reshape(480, 512), TN, preferred_element_type=F32))
    forward(1, gd_z, gd_c)
    forward(2, ud_z, ud_c)
    deltas = [swap_dp(q) for q in range(3)]
    arrive(gd_c)
    arrive(ud_c)
    back = jnp.concatenate([rows(1, dp), rows(2, dp)], axis=0)
    in_x = x_scatter(1, lax.dot_general(back, W[0:2].reshape(960, 512), TN, preferred_element_type=F32))
    out_y = y_scatter(0, out_x)
    in_y = y_scatter(1, in_x)

    fwd = []
    for q in range(3):
        arrive(deltas[q])
        fwd.append(send(D.at[q, odp, c], D.at[q, odp, c], core))
    arrive(other_y)
    arrive(other_x)
    done = []
    for q, ref in ((0, dg_ref), (1, gg_ref), (2, ug_ref)):
        arrive([fwd[q]])
        right = T[1 if q == 0 else 0].reshape(1024, 512)
        for h in range(2):
            left = jnp.concatenate([D[q, d, h, j] for d in range(2) for j in range(4)], axis=1)
            value = lax.dot_general(left, right, NN, preferred_element_type=F32).astype(BF)
            if h == 0:
                WG[q, 0:HALF] = value
            else:
                WG[q, HALF : HALF + LAST] = value[0:LAST]
        done.append(local(WG.at[q], ref))
    done.append(finish(0, out_y, out_ref))
    done.append(finish(1, in_y, ing_ref))
    for copy in sent:
        copy.wait_send()
    for copy in done:
        copy.wait()


def body(tokens, gate_weight, up_weight, down_weight, out_grad):
    any_spec = pl.BlockSpec(memory_space=pl.ANY)
    small = jax.ShapeDtypeStruct((16, 512), BF)
    large = jax.ShapeDtypeStruct((464, 512), BF)
    output, input_grad, gate_t, up_t, down_grad = pl.pallas_call(
        kernel,
        out_shape=(small, small, large, large, large),
        in_specs=[any_spec] * 5,
        out_specs=(any_spec,) * 5,
        scratch_shapes=[
            pltpu.VMEM((2, 2, 8, 4, 16, 512), BF),
            pltpu.VMEM((3, 2, HALF, 512), BF),
            pltpu.VMEM((3, 4, HALF, 128), F32),
            pltpu.VMEM((3, 4, HALF, 128), BF),
            pltpu.VMEM((3, 4, HALF, 128), BF),
            pltpu.VMEM((3, 3, HALF, 128), BF),
            pltpu.VMEM((3, 3, HALF, 128), BF),
            pltpu.VMEM((2, HALF, 128), F32),
            pltpu.VMEM((3, 2, 2, 4, HALF, 128), BF),
            pltpu.VMEM((2, 8, 4, 16, 512), BF),
            pltpu.VMEM((2, 3, 8, 16, 512), BF),
            pltpu.VMEM((2, 8, 16, 512), BF),
            pltpu.VMEM((2, 7, 16, 512), BF),
            pltpu.VMEM((3, 464, 512), BF),
            pltpu.VMEM((2, 16, 512), BF),
            pltpu.SemaphoreType.DMA((16,)),
            pltpu.SemaphoreType.DMA((128,)),
            pltpu.SemaphoreType.DMA((128,)),
        ],
        compiler_params=pltpu.CompilerParams(
            collective_id=0, has_side_effects=True, vmem_limit_bytes=48 * 2**20
        ),
        name="block",
    )(tokens, out_grad, gate_weight.T, up_weight.T, down_weight)
    return output, input_grad, gate_t.T, up_t.T, down_grad


def solution(mesh):
    placed = (
        P(("dp", "gx", "gy"), "gz"),
        P("gz", ("gx", "gy")),
        P("gz", ("gx", "gy")),
        P(("gx", "gy"), "gz"),
        P(("dp", "gx", "gy"), "gz"),
    )
    return jax.shard_map(
        body,
        mesh=mesh,
        in_specs=placed,
        out_specs=(
            P(("dp", "gx", "gy"), "gz"),
            P(("dp", "gx", "gy"), "gz"),
            P("gz", ("gx", "gy")),
            P("gz", ("gx", "gy")),
            P(("gx", "gy"), "gz"),
        ),
        check_vma=False,
    )
```

```python
import jax
import jax.numpy as jnp
from jax import lax
from jax.experimental import pallas as pl
from jax.experimental.pallas import tpu as pltpu
from jax.sharding import PartitionSpec as P

BF = jnp.bfloat16
F32 = jnp.float32
HALF = 240
LAST = 224
CUT = 128
NT = (((1,), (1,)), ((), ()))
TN = (((0,), (0,)), ((), ()))
NN = (((1,), (0,)), ((), ()))
FAR = (4, 3, 5, 2, 6, 1, 7)


def kernel(
    tok_ref, grad_ref, wg_ref, wu_ref, wd_ref,
    out_ref, ing_ref, gg_ref, ug_ref, dg_ref,
    T, W, PM, SC, RC, SZ, RA, RZ, V, D, OB, RX, SY, RY, WG, FO,
    lsem, ssem, rsem,
):
    dp, gx, gy, gz = (lax.axis_index(a) for a in ("dp", "gx", "gy", "gz"))
    zh, c = lax.div(gz, 2), lax.rem(gz, 2)
    z = 2 * zh + dp
    other = 1 - c
    odp = 1 - dp

    def ydev(k):
        return (dp, lax.rem(gx + k, 8), gy, gz)

    def xdev(k):
        return (dp, gx, lax.rem(gy + k, 4), gz)

    def zdev(k):
        there = lax.rem(z + k + 8, 8)
        return (lax.rem(there, 2), gx, gy, lax.div(there, 2) * 2 + c)

    core = (dp, gx, gy, zh * 2 + other)
    partner = (odp, gx, gy, gz)

    count = [0]
    sent = []

    def send(src, dst, device):
        i = count[0]
        count[0] += 1
        copy = pltpu.make_async_remote_copy(
            src_ref=src,
            dst_ref=dst,
            send_sem=ssem.at[i],
            recv_sem=rsem.at[i],
            device_id=device,
            device_id_type=pl.DeviceIdType.MESH,
        )
        copy.start()
        sent.append(copy)
        return copy

    def arrive(copies):
        for copy in copies:
            copy.wait_recv()

    lcount = [0]

    def local(src, dst):
        i = lcount[0]
        lcount[0] += 1
        copy = pltpu.make_async_copy(src, dst, lsem.at[i])
        copy.start()
        return copy

    tok_in = [local(tok_ref, T.at[0, dp, gx, gy]), local(grad_ref, T.at[1, dp, gx, gy])]
    w_in = []
    for q, ref in enumerate((wg_ref, wu_ref, wd_ref)):
        w_in.append(local(ref.at[pl.ds(0, HALF)], W.at[q, 0]))
        w_in.append(local(ref.at[pl.ds(HALF, LAST)], W.at[q, 1, pl.ds(0, LAST)]))

    barrier = pltpu.get_barrier_semaphore()
    partners = [ydev(k) for k in FAR] + [xdev(k) for k in (2, 1, 3)]
    partners += [zdev(k) for k in (2, -2, 1, -1)] + [core]
    for device in partners:
        pl.semaphore_signal(barrier, inc=1, device_id=device, device_id_type=pl.DeviceIdType.MESH)
    for q in range(3):
        W[q, 1, LAST:, :] = jnp.zeros((HALF - LAST, 512), BF)
    for copy in tok_in:
        copy.wait()
    pl.semaphore_wait(barrier, len(partners))

    def ysends(a, d, whole):
        ref = T.at[a, d, gx] if whole else T.at[a, d, gx, gy]
        return {k: send(ref, ref, ydev(k)) for k in FAR}

    def xsends(ref):
        return [send(ref, ref, xdev(k)) for k in (2, 1, 3)]

    tok_y = ysends(0, dp, False)
    tok_x = xsends(T.at[0, dp, gx, gy])
    grad_x = xsends(T.at[1, dp, gx, gy])
    swap = [send(T.at[a, dp, gx, gy], T.at[a, dp, gx, gy], partner) for a in range(2)]
    for copy in w_in:
        copy.wait()
    for k in (1, 7, 2, 6, 3, 5, 4):
        tok_y[k].wait_recv()
        tok_x += xsends(T.at[0, dp, lax.rem(gx + 8 - k, 8), gy])
        if k == 7:
            arrive(grad_x)
            grad_y = ysends(1, dp, True)
    arrive(tok_x)

    def project(q, x):
        far = lax.dot_general(W[q, other], x, NT, preferred_element_type=F32)
        for j in range(4):
            SC[q, j] = far[:, 128 * j : 128 * j + 128].astype(BF)
        copy = send(SC.at[q], RC.at[q], core)
        mine = lax.dot_general(W[q, c], x, NT, preferred_element_type=F32)
        for j in range(4):
            PM[q, j] = mine[:, 128 * j : 128 * j + 128]
        return copy

    def chunk(q, k):
        j = lax.rem(zh + k, 4)
        return PM[q, j] + RC[q, j].astype(F32)

    low, high = pl.ds(0, CUT), pl.ds(CUT, HALF - CUT)

    def scatter(q, copy):
        copy.wait_recv()
        SZ[q, 1] = chunk(q, 2).astype(BF)
        first = [
            send(SZ.at[q, 1, low], RA.at[q, low], zdev(2)),
            send(SZ.at[q, 1, high], RA.at[q, high], zdev(-2)),
        ]
        SZ[q, 0, CUT:] = chunk(q, 1)[CUT:].astype(BF)
        SZ[q, 2, :CUT] = chunk(q, 3)[:CUT].astype(BF)
        second = [
            send(SZ.at[q, 0, high], RZ.at[q, 0, high], zdev(2)),
            send(SZ.at[q, 2, low], RZ.at[q, 1, low], zdev(-2)),
        ]
        return first, second

    def relay(q, copies):
        first, second = copies
        first[0].wait_recv()
        SZ[q, 0, :CUT] = (chunk(q, 1)[:CUT] + RA[q, :CUT].astype(F32)).astype(BF)
        second.append(send(SZ.at[q, 0, low], RZ.at[q, 0, low], zdev(2)))
        first[1].wait_recv()
        SZ[q, 2, CUT:] = (chunk(q, 3)[CUT:] + RA[q, CUT:].astype(F32)).astype(BF)
        second.append(send(SZ.at[q, 2, high], RZ.at[q, 1, high], zdev(-2)))

    def total(q, copies):
        arrive(copies[1])
        return chunk(q, 0) + RZ[q, 0].astype(F32) + RZ[q, 1].astype(F32)

    x = T[0, dp].reshape(512, 512)
    gate_c = project(0, x)
    up_c = project(1, x)
    gate_z = scatter(0, gate_c)
    up_z = scatter(1, up_c)
    arrive(swap)
    other_y = ysends(0, odp, False)
    other_x = xsends(T.at[1, odp, gx, gy])
    relay(0, gate_z)
    relay(1, up_z)
    arrive(grad_y.values())
    hg_c = project(2, T[1, dp].reshape(512, 512))
    hg_z = scatter(2, hg_c)
    arrive(other_x)
    other_x = list(ysends(1, odp, True).values())
    arrive(other_y.values())
    other_y = xsends(T.at[0, odp, :, gy])
    relay(2, hg_z)

    right, left, to_core = {}, {}, {}

    def spread(q, value):
        D[q, c, z] = value.astype(BF)
        ref = D.at[q, c, z]
        right[q] = send(ref, ref, zdev(1))
        left[q] = send(ref, ref, zdev(-1))
        to_core[q] = [send(ref, ref, core)]

    def step(q, s):
        there, back = lax.rem(z + 8 - s, 8), lax.rem(z + s, 8)
        a, b = D.at[q, c, there], D.at[q, c, back]
        right[q].wait_recv()
        if s < 4:
            a_next = a if s < 3 else D.at[q, c, there, low]
            right[q] = send(a_next, a_next, zdev(1))
            to_core[q].append(send(a, a, core))
        left[q].wait_recv()
        if s < 4:
            b_next = b if s < 3 else D.at[q, c, back, high]
            left[q] = send(b_next, b_next, zdev(-1))
        to_core[q].append(send(b, b, core))

    def rows(q, d):
        halves = [
            jnp.concatenate([D[q, h, 2 * j + d] for j in range(4)], axis=1) for h in range(2)
        ]
        return jnp.concatenate(halves, axis=0)

    def x_scatter(o, part):
        part = part.astype(BF).reshape(8, 4, 16, 512)
        for g in range(8):
            OB[o, lax.rem(g + 14 - gx, 8)] = part[g]
        groups = []
        for h in range(2):
            block = pl.ds(4 * h, 4)
            groups.append([
                send(OB.at[o, block, lax.rem(gy + k, 4)], RX.at[o, k - 1, block], xdev(k))
                for k in (2, 1, 3)
            ])
        return groups

    def y_scatter(o, h, copies):
        arrive(copies[h])
        block = slice(4 * h, 4 * h + 4)
        value = OB[o, block, gy].astype(F32)
        for k in range(3):
            value = value + RX[o, k, block].astype(F32)
        SY[o, block] = value.astype(BF)
        order = (2, 1, 3, 0) if h == 0 else (4, 5, 7)
        return [send(SY.at[o, i], RY.at[o, (i + 2) % 8 - 1], ydev((i + 2) % 8)) for i in order]

    def finish(o, copies, ref):
        arrive(copies)
        value = SY[o, 6].astype(F32)
        for k in range(7):
            value = value + RY[o, k].astype(F32)
        FO[o] = value.astype(BF)
        return local(FO.at[o], ref)

    gate_val = total(0, gate_z)
    up_val = total(1, up_z)
    gate_sig = jax.nn.sigmoid(gate_val)
    gate_act = gate_val * gate_sig
    V[0] = up_val * gate_sig * (1.0 + gate_val * (1.0 - gate_sig))
    V[1] = gate_act
    spread(0, gate_act * up_val)
    step(0, 1)
    hid_grad = total(2, hg_z)
    spread(1, hid_grad * V[0])
    spread(2, hid_grad * V[1])
    step(0, 2)
    step(1, 1)
    step(2, 1)
    step(0, 3)
    step(1, 2)
    step(2, 2)
    step(0, 4)
    step(1, 3)
    step(2, 3)
    arrive(to_core[0])
    part = lax.dot_general(rows(0, dp), W[2].reshape(480, 512), TN, preferred_element_type=F32)
    out_x = x_scatter(0, part)
    step(1, 4)
    step(2, 4)
    arrive(to_core[1])
    arrive(to_core[2])
    both = jnp.concatenate([rows(1, dp), rows(2, dp)], axis=0)
    part = lax.dot_general(both, W[0:2].reshape(960, 512), TN, preferred_element_type=F32)
    in_x = x_scatter(1, part)
    out_y = y_scatter(0, 0, out_x) + y_scatter(0, 1, out_x)

    done = []

    def weight_grad(q, ref):
        right = T[1 if q == 0 else 0].reshape(1024, 512)
        for h in range(2):
            left = jnp.concatenate([D[q, h, 2 * j + d] for d in range(2) for j in range(4)], axis=1)
            value = lax.dot_general(left, right, NN, preferred_element_type=F32).astype(BF)
            if h == 0:
                WG[q, 0:HALF] = value
            else:
                WG[q, HALF : HALF + LAST] = value[0:LAST]
        done.append(local(WG.at[q], ref))

    arrive(other_y)
    arrive(other_x)
    weight_grad(0, dg_ref)
    in_y = y_scatter(1, 0, in_x)
    in_y += y_scatter(1, 1, in_x)
    weight_grad(1, gg_ref)
    weight_grad(2, ug_ref)
    done.append(finish(0, out_y, out_ref))
    done.append(finish(1, in_y, ing_ref))
    for copy in sent:
        copy.wait_send()
    for copy in done:
        copy.wait()


def store(*refs):
    n = (len(refs) - 1) // 3
    held, sem = refs[2 * n : 3 * n], refs[-1]
    fetch = [pltpu.make_async_copy(refs[i], held[i], sem.at[i]) for i in range(n)]
    put = [pltpu.make_async_copy(held[i], refs[n + i], sem.at[n + i]) for i in range(n)]
    for copy in fetch:
        copy.start()
    for i in range(n):
        fetch[i].wait()
        put[i].start()
    for copy in put:
        copy.wait()


def body(tokens, gate_weight, up_weight, down_weight, out_grad):
    any_spec = pl.BlockSpec(memory_space=pl.ANY)
    hbm_spec = pl.BlockSpec(memory_space=pltpu.HBM)
    small = jax.ShapeDtypeStruct((16, 512), BF)
    large = jax.ShapeDtypeStruct((464, 512), BF)
    results = pl.pallas_call(
        kernel,
        out_shape=(small, small, large, large, large),
        in_specs=[hbm_spec] * 5,
        out_specs=(any_spec,) * 5,
        scratch_shapes=[
            pltpu.VMEM((2, 2, 8, 4, 16, 512), BF),
            pltpu.VMEM((3, 2, HALF, 512), BF),
            pltpu.VMEM((3, 4, HALF, 128), F32),
            pltpu.VMEM((3, 4, HALF, 128), BF),
            pltpu.VMEM((3, 4, HALF, 128), BF),
            pltpu.VMEM((3, 3, HALF, 128), BF),
            pltpu.VMEM((3, HALF, 128), BF),
            pltpu.VMEM((3, 2, HALF, 128), BF),
            pltpu.VMEM((2, HALF, 128), F32),
            pltpu.VMEM((3, 2, 8, HALF, 128), BF),
            pltpu.VMEM((2, 8, 4, 16, 512), BF),
            pltpu.VMEM((2, 3, 8, 16, 512), BF),
            pltpu.VMEM((2, 8, 16, 512), BF),
            pltpu.VMEM((2, 7, 16, 512), BF),
            pltpu.VMEM((3, 464, 512), BF),
            pltpu.VMEM((2, 16, 512), BF),
            pltpu.SemaphoreType.DMA((16,)),
            pltpu.SemaphoreType.DMA((176,)),
            pltpu.SemaphoreType.DMA((176,)),
        ],
        compiler_params=pltpu.CompilerParams(
            collective_id=0, has_side_effects=True, vmem_limit_bytes=62 * 2**20
        ),
        name="block",
    )(tokens, out_grad, gate_weight.T, up_weight.T, down_weight)
    output, input_grad, gate_t, up_t, down_grad = pl.pallas_call(
        store,
        out_shape=(small, small, large, large, large),
        in_specs=[any_spec] * 5,
        out_specs=(hbm_spec,) * 5,
        scratch_shapes=[pltpu.VMEM(r.shape, BF) for r in results] + [pltpu.SemaphoreType.DMA((10,))],
        compiler_params=pltpu.CompilerParams(vmem_limit_bytes=62 * 2**20),
        name="store",
    )(*results)
    return output, input_grad, gate_t.T, up_t.T, down_grad


def solution(mesh):
    placed = (
        P(("dp", "gx", "gy"), "gz"),
        P("gz", ("gx", "gy")),
        P("gz", ("gx", "gy")),
        P(("gx", "gy"), "gz"),
        P(("dp", "gx", "gy"), "gz"),
    )
    return jax.shard_map(
        body,
        mesh=mesh,
        in_specs=placed,
        out_specs=(
            P(("dp", "gx", "gy"), "gz"),
            P(("dp", "gx", "gy"), "gz"),
            P("gz", ("gx", "gy")),
            P("gz", ("gx", "gy")),
            P(("gx", "gy"), "gz"),
        ),
        check_vma=False,
    )
```

```python
import jax
import jax.numpy as jnp
from jax import lax
from jax.experimental import pallas as pl
from jax.experimental.pallas import tpu as pltpu
from jax.sharding import PartitionSpec as P

BF = jnp.bfloat16
F32 = jnp.float32
HALF = 240
LAST = 224
CUT = 128
NT = (((1,), (1,)), ((), ()))
TN = (((0,), (0,)), ((), ()))
NN = (((1,), (0,)), ((), ()))
FAR = (4, 3, 5, 2, 6, 1, 7)


def kernel(
    tok_ref, grad_ref, wg_ref, wu_ref, wd_ref,
    out_ref, ing_ref, gg_ref, ug_ref, dg_ref,
    T, W, PM, SC, RC, SZ, RA, RZ, V, D, OB, RX, SY, RY, WG, FO,
    lsem, ssem, rsem,
):
    dp, gx, gy, gz = (lax.axis_index(a) for a in ("dp", "gx", "gy", "gz"))
    zh, c = lax.div(gz, 2), lax.rem(gz, 2)
    z = 2 * zh + dp
    other = 1 - c
    odp = 1 - dp

    def ydev(k):
        return (dp, lax.rem(gx + k, 8), gy, gz)

    def xdev(k):
        return (dp, gx, lax.rem(gy + k, 4), gz)

    def zdev(k):
        there = lax.rem(z + k + 8, 8)
        return (lax.rem(there, 2), gx, gy, lax.div(there, 2) * 2 + c)

    core = (dp, gx, gy, zh * 2 + other)
    partner = (odp, gx, gy, gz)

    count = [0]
    sent = []

    def send(src, dst, device):
        i = count[0]
        count[0] += 1
        copy = pltpu.make_async_remote_copy(
            src_ref=src,
            dst_ref=dst,
            send_sem=ssem.at[i],
            recv_sem=rsem.at[i],
            device_id=device,
            device_id_type=pl.DeviceIdType.MESH,
        )
        copy.start()
        sent.append(copy)
        return copy

    def arrive(copies):
        for copy in copies:
            copy.wait_recv()

    lcount = [0]

    def local(src, dst):
        i = lcount[0]
        lcount[0] += 1
        copy = pltpu.make_async_copy(src, dst, lsem.at[i])
        copy.start()
        return copy

    tok_in = [local(tok_ref, T.at[0, dp, gx, gy]), local(grad_ref, T.at[1, dp, gx, gy])]
    w_in = []
    for q, ref in enumerate((wg_ref, wu_ref, wd_ref)):
        w_in.append(local(ref.at[pl.ds(0, HALF)], W.at[q, 0]))
        w_in.append(local(ref.at[pl.ds(HALF, LAST)], W.at[q, 1, pl.ds(0, LAST)]))

    barrier = pltpu.get_barrier_semaphore()
    partners = [ydev(k) for k in FAR] + [xdev(k) for k in (2, 1, 3)]
    partners += [zdev(k) for k in (2, -2, 1, -1)] + [core]
    for device in partners:
        pl.semaphore_signal(barrier, inc=1, device_id=device, device_id_type=pl.DeviceIdType.MESH)
    for q in range(3):
        W[q, 1, LAST:, :] = jnp.zeros((HALF - LAST, 512), BF)
    for copy in tok_in:
        copy.wait()
    pl.semaphore_wait(barrier, len(partners))

    def ysends(a, d):
        ref = T.at[a, d, gx, gy]
        return {k: send(ref, ref, ydev(k)) for k in FAR}

    def xsends(ref):
        return [send(ref, ref, xdev(k)) for k in (2, 1, 3)]

    def pass_on(a):
        for k in (1, 7, 2, 6, 3, 5, 4):
            ys[a][k].wait_recv()
            xs[a] += xsends(T.at[a, dp, lax.rem(gx + 8 - k, 8), gy])

    ys, xs = {}, {}
    ys[0] = ysends(0, dp)
    xs[0] = xsends(T.at[0, dp, gx, gy])
    ys[1] = ysends(1, dp)
    for copy in w_in:
        copy.wait()
    pass_on(0)
    xs[1] = xsends(T.at[1, dp, gx, gy])
    swap = [send(T.at[a, dp, gx, gy], T.at[a, dp, gx, gy], partner) for a in range(2)]
    arrive(xs[0])

    def project(q, x):
        far = lax.dot_general(W[q, other], x, NT, preferred_element_type=F32)
        for j in range(4):
            SC[q, j] = far[:, 128 * j : 128 * j + 128].astype(BF)
        copy = send(SC.at[q], RC.at[q], core)
        mine = lax.dot_general(W[q, c], x, NT, preferred_element_type=F32)
        for j in range(4):
            PM[q, j] = mine[:, 128 * j : 128 * j + 128]
        return copy

    def chunk(q, k):
        j = lax.rem(zh + k, 4)
        return PM[q, j] + RC[q, j].astype(F32)

    low, high = pl.ds(0, CUT), pl.ds(CUT, HALF - CUT)

    def scatter(q, copy):
        copy.wait_recv()
        SZ[q, 1] = chunk(q, 2).astype(BF)
        first = [
            send(SZ.at[q, 1, low], RA.at[q, low], zdev(2)),
            send(SZ.at[q, 1, high], RA.at[q, high], zdev(-2)),
        ]
        SZ[q, 0, CUT:] = chunk(q, 1)[CUT:].astype(BF)
        SZ[q, 2, :CUT] = chunk(q, 3)[:CUT].astype(BF)
        second = [
            send(SZ.at[q, 0, high], RZ.at[q, 0, high], zdev(2)),
            send(SZ.at[q, 2, low], RZ.at[q, 1, low], zdev(-2)),
        ]
        return first, second

    def relay(q, copies):
        first, second = copies
        first[0].wait_recv()
        SZ[q, 0, :CUT] = (chunk(q, 1)[:CUT] + RA[q, :CUT].astype(F32)).astype(BF)
        second.append(send(SZ.at[q, 0, low], RZ.at[q, 0, low], zdev(2)))
        first[1].wait_recv()
        SZ[q, 2, CUT:] = (chunk(q, 3)[CUT:] + RA[q, CUT:].astype(F32)).astype(BF)
        second.append(send(SZ.at[q, 2, high], RZ.at[q, 1, high], zdev(-2)))

    def total(q, copies):
        arrive(copies[1])
        return chunk(q, 0) + RZ[q, 0].astype(F32) + RZ[q, 1].astype(F32)

    x = T[0, dp].reshape(512, 512)
    gate_c = project(0, x)
    up_c = project(1, x)
    gate_z = scatter(0, gate_c)
    up_z = scatter(1, up_c)
    pass_on(1)
    arrive(swap)
    other_y = [copy for a in range(2) for copy in ysends(a, odp).values()]
    relay(0, gate_z)
    relay(1, up_z)
    arrive(xs[1])
    hg_c = project(2, T[1, dp].reshape(512, 512))
    hg_z = scatter(2, hg_c)
    arrive(other_y)
    other_x = [copy for a in range(2) for copy in xsends(T.at[a, odp, :, gy])]

    right, left, to_core = {}, {}, {}
    near_b = zdev(2 * dp - 1)

    def spread(q, value):
        D[q, dp, c, zh] = value.astype(BF)
        ref = D.at[q, dp, c, zh]
        right[q] = send(ref, ref, zdev(2))
        left[q] = send(ref, ref, zdev(-2))
        to_core[q] = [send(ref, ref, core)]

    def spread_on(q):
        there, back = lax.rem(zh + 3, 4), lax.rem(zh + 1, 4)
        right[q].wait_recv()
        ref = D.at[q, dp, c, there, low]
        right[q] = send(ref, ref, zdev(2))
        ref = D.at[q, dp, c, there]
        to_core[q].append(send(ref, ref, core))
        left[q].wait_recv()
        ref = D.at[q, dp, c, back, high]
        left[q] = send(ref, ref, zdev(-2))
        ref = D.at[q, dp, c, back]
        to_core[q].append(send(ref, ref, core))

    def spread_end(q):
        right[q].wait_recv()
        left[q].wait_recv()
        ref = D.at[q, dp, c, lax.rem(zh + 2, 4)]
        to_core[q].append(send(ref, ref, core))

    def swap_replicas(q):
        refs = [D.at[q, dp, c, lax.rem(zh + 4 + k, 4)] for k in (0, 2 * dp - 1, 1 - 2 * dp)]
        return [
            send(refs[0], refs[0], partner),
            send(refs[0], refs[0], near_b),
            send(refs[1], refs[1], partner),
            send(refs[2], refs[2], near_b),
        ]

    def rows(q, d):
        halves = [
            jnp.concatenate([D[q, d, h, j] for j in range(4)], axis=1) for h in range(2)
        ]
        return jnp.concatenate(halves, axis=0)

    def x_scatter(o, part):
        part = part.astype(BF).reshape(8, 4, 16, 512)
        for g in range(8):
            OB[o, lax.rem(g + 14 - gx, 8)] = part[g]
        groups = []
        for h in range(2):
            block = pl.ds(4 * h, 4)
            groups.append([
                send(OB.at[o, block, lax.rem(gy + k, 4)], RX.at[o, k - 1, block], xdev(k))
                for k in (2, 1, 3)
            ])
        return groups

    def y_scatter(o, h, copies):
        arrive(copies[h])
        block = slice(4 * h, 4 * h + 4)
        value = OB[o, block, gy].astype(F32)
        for k in range(3):
            value = value + RX[o, k, block].astype(F32)
        SY[o, block] = value.astype(BF)
        order = (2, 1, 3, 0) if h == 0 else (4, 5, 7)
        return [send(SY.at[o, i], RY.at[o, (i + 2) % 8 - 1], ydev((i + 2) % 8)) for i in order]

    def finish(o, copies, ref):
        arrive(copies)
        value = SY[o, 6].astype(F32)
        for k in range(7):
            value = value + RY[o, k].astype(F32)
        FO[o] = value.astype(BF)
        return local(FO.at[o], ref)

    gate_val = total(0, gate_z)
    up_val = total(1, up_z)
    gate_sig = jax.nn.sigmoid(gate_val)
    gate_act = gate_val * gate_sig
    V[0] = up_val * gate_sig * (1.0 + gate_val * (1.0 - gate_sig))
    V[1] = gate_act
    spread(0, gate_act * up_val)
    relay(2, hg_z)
    spread_on(0)
    hid_grad = total(2, hg_z)
    spread(1, hid_grad * V[0])
    spread(2, hid_grad * V[1])
    spread_end(0)
    arrive(to_core[0])
    part = lax.dot_general(rows(0, dp), W[2].reshape(480, 512), TN, preferred_element_type=F32)
    out_x = x_scatter(0, part)
    spread_on(1)
    spread_on(2)
    swapped = [swap_replicas(q) for q in range(3)]
    spread_end(1)
    spread_end(2)
    arrive(to_core[1])
    arrive(to_core[2])
    both = jnp.concatenate([rows(1, dp), rows(2, dp)], axis=0)
    part = lax.dot_general(both, W[0:2].reshape(960, 512), TN, preferred_element_type=F32)
    in_x = x_scatter(1, part)
    out_y = y_scatter(0, 0, out_x) + y_scatter(0, 1, out_x)

    done = []

    def weight_grad(q, ref):
        right = T[1 if q == 0 else 0].reshape(1024, 512)
        for h in range(2):
            left = jnp.concatenate([D[q, d, h, j] for d in range(2) for j in range(4)], axis=1)
            value = lax.dot_general(left, right, NN, preferred_element_type=F32).astype(BF)
            if h == 0:
                WG[q, 0:HALF] = value
            else:
                WG[q, HALF : HALF + LAST] = value[0:LAST]
        done.append(local(WG.at[q], ref))

    in_y = y_scatter(1, 0, in_x)
    in_y += y_scatter(1, 1, in_x)
    late = []
    for q in range(3):
        arrive(swapped[q])
        ref = D.at[q, odp, c]
        late.append(send(ref, ref, core))
    arrive(other_x)
    for q, ref in enumerate((dg_ref, gg_ref, ug_ref)):
        arrive([late[q]])
        weight_grad(q, ref)
    done.append(finish(0, out_y, out_ref))
    done.append(finish(1, in_y, ing_ref))
    for copy in sent:
        copy.wait_send()
    for copy in done:
        copy.wait()


def store(*refs):
    n = (len(refs) - 1) // 3
    sem = refs[-1]
    fetch, put = [], []
    for i in range(n):
        source, result, held = refs[i], refs[n + i], refs[2 * n + i]
        size = source.shape[0]
        cuts = [0, 160, 320, size] if size > 160 else [0, size]
        for start, stop in zip(cuts[:-1], cuts[1:], strict=True):
            rows, k = pl.ds(start, stop - start), len(fetch)
            fetch.append(pltpu.make_async_copy(source.at[rows], held.at[rows], sem.at[0, k]))
            put.append(pltpu.make_async_copy(held.at[rows], result.at[rows], sem.at[1, k]))
    for copy in fetch:
        copy.start()
    for into, out in zip(fetch, put, strict=True):
        into.wait()
        out.start()
    for copy in put:
        copy.wait()


def body(tokens, gate_weight, up_weight, down_weight, out_grad):
    any_spec = pl.BlockSpec(memory_space=pl.ANY)
    hbm_spec = pl.BlockSpec(memory_space=pltpu.HBM)
    small = jax.ShapeDtypeStruct((16, 512), BF)
    large = jax.ShapeDtypeStruct((464, 512), BF)
    results = pl.pallas_call(
        kernel,
        out_shape=(small, small, large, large, large),
        in_specs=[hbm_spec] * 5,
        out_specs=(any_spec,) * 5,
        scratch_shapes=[
            pltpu.VMEM((2, 2, 8, 4, 16, 512), BF),
            pltpu.VMEM((3, 2, HALF, 512), BF),
            pltpu.VMEM((3, 4, HALF, 128), F32),
            pltpu.VMEM((3, 4, HALF, 128), BF),
            pltpu.VMEM((3, 4, HALF, 128), BF),
            pltpu.VMEM((3, 3, HALF, 128), BF),
            pltpu.VMEM((3, HALF, 128), BF),
            pltpu.VMEM((3, 2, HALF, 128), BF),
            pltpu.VMEM((2, HALF, 128), F32),
            pltpu.VMEM((3, 2, 2, 4, HALF, 128), BF),
            pltpu.VMEM((2, 8, 4, 16, 512), BF),
            pltpu.VMEM((2, 3, 8, 16, 512), BF),
            pltpu.VMEM((2, 8, 16, 512), BF),
            pltpu.VMEM((2, 7, 16, 512), BF),
            pltpu.VMEM((3, 464, 512), BF),
            pltpu.VMEM((2, 16, 512), BF),
            pltpu.SemaphoreType.DMA((16,)),
            pltpu.SemaphoreType.DMA((208,)),
            pltpu.SemaphoreType.DMA((208,)),
        ],
        compiler_params=pltpu.CompilerParams(
            collective_id=0, has_side_effects=True, vmem_limit_bytes=62 * 2**20
        ),
        name="block",
    )(tokens, out_grad, gate_weight.T, up_weight.T, down_weight)
    output, input_grad, gate_t, up_t, down_grad = pl.pallas_call(
        store,
        out_shape=(small, small, large, large, large),
        in_specs=[any_spec] * 5,
        out_specs=(hbm_spec,) * 5,
        scratch_shapes=[pltpu.VMEM(r.shape, BF) for r in results] + [pltpu.SemaphoreType.DMA((2, 11))],
        compiler_params=pltpu.CompilerParams(vmem_limit_bytes=62 * 2**20),
        name="store",
    )(*results)
    return output, input_grad, gate_t.T, up_t.T, down_grad


def solution(mesh):
    placed = (
        P(("dp", "gx", "gy"), "gz"),
        P("gz", ("gx", "gy")),
        P("gz", ("gx", "gy")),
        P(("gx", "gy"), "gz"),
        P(("dp", "gx", "gy"), "gz"),
    )
    return jax.shard_map(
        body,
        mesh=mesh,
        in_specs=placed,
        out_specs=(
            P(("dp", "gx", "gy"), "gz"),
            P(("dp", "gx", "gy"), "gz"),
            P("gz", ("gx", "gy")),
            P("gz", ("gx", "gy")),
            P(("gx", "gy"), "gz"),
        ),
        check_vma=False,
    )
```

```python
import jax
import jax.numpy as jnp
from jax import lax
from jax.experimental import pallas as pl
from jax.experimental.pallas import tpu as pltpu
from jax.sharding import PartitionSpec as P

BF = jnp.bfloat16
F32 = jnp.float32
HALF = 240
LAST = 224
CUT = 128
NT = (((1,), (1,)), ((), ()))
TN = (((0,), (0,)), ((), ()))
NN = (((1,), (0,)), ((), ()))
FAR = (4, 3, 5, 2, 6, 1, 7)


def kernel(
    tok_ref, grad_ref, wg_ref, wu_ref, wd_ref,
    out_ref, ing_ref, gg_ref, ug_ref, dg_ref,
    T, W, PM, SC, RC, SZ, RA, RZ, V, D, OB, RX, SY, RY, WG, FO,
    lsem, ssem, rsem,
):
    dp, gx, gy, gz = (lax.axis_index(a) for a in ("dp", "gx", "gy", "gz"))
    zh, c = lax.div(gz, 2), lax.rem(gz, 2)
    z = 2 * zh + dp
    other = 1 - c
    odp = 1 - dp

    def ydev(k):
        return (dp, lax.rem(gx + k, 8), gy, gz)

    def xdev(k):
        return (dp, gx, lax.rem(gy + k, 4), gz)

    def zdev(k):
        there = lax.rem(z + k + 8, 8)
        return (lax.rem(there, 2), gx, gy, lax.div(there, 2) * 2 + c)

    core = (dp, gx, gy, zh * 2 + other)
    partner = (odp, gx, gy, gz)

    count = [0]
    sent = []

    def send(src, dst, device):
        i = count[0]
        count[0] += 1
        copy = pltpu.make_async_remote_copy(
            src_ref=src,
            dst_ref=dst,
            send_sem=ssem.at[i],
            recv_sem=rsem.at[i],
            device_id=device,
            device_id_type=pl.DeviceIdType.MESH,
        )
        copy.start()
        sent.append(copy)
        return copy

    def arrive(copies):
        for copy in copies:
            copy.wait_recv()

    lcount = [0]

    def local(src, dst):
        i = lcount[0]
        lcount[0] += 1
        copy = pltpu.make_async_copy(src, dst, lsem.at[i])
        copy.start()
        return copy

    tok_in = [local(tok_ref, T.at[0, dp, gx, gy]), local(grad_ref, T.at[1, dp, gx, gy])]
    w_in = []
    for q, ref in enumerate((wg_ref, wu_ref, wd_ref)):
        w_in.append(local(ref.at[pl.ds(0, HALF)], W.at[q, 0]))
        w_in.append(local(ref.at[pl.ds(HALF, LAST)], W.at[q, 1, pl.ds(0, LAST)]))

    barrier = pltpu.get_barrier_semaphore()
    partners = [ydev(k) for k in FAR] + [xdev(k) for k in (2, 1, 3)]
    partners += [zdev(k) for k in (2, -2, 1, -1)] + [core]
    for device in partners:
        pl.semaphore_signal(barrier, inc=1, device_id=device, device_id_type=pl.DeviceIdType.MESH)
    for q in range(3):
        W[q, 1, LAST:, :] = jnp.zeros((HALF - LAST, 512), BF)
    for copy in tok_in:
        copy.wait()
    pl.semaphore_wait(barrier, len(partners))

    def ysends(a, d):
        ref = T.at[a, d, gx, gy]
        return {k: send(ref, ref, ydev(k)) for k in FAR}

    def xsends(ref):
        return [send(ref, ref, xdev(k)) for k in (2, 1, 3)]

    def pass_on(a):
        for k in (1, 7, 2, 6, 3, 5, 4):
            ys[a][k].wait_recv()
            xs[a] += xsends(T.at[a, dp, lax.rem(gx + 8 - k, 8), gy])

    ys, xs = {}, {}
    ys[0] = ysends(0, dp)
    xs[0] = xsends(T.at[0, dp, gx, gy])
    ys[1] = ysends(1, dp)
    for copy in w_in:
        copy.wait()
    pass_on(0)
    xs[1] = xsends(T.at[1, dp, gx, gy])
    swap = [send(T.at[a, dp, gx, gy], T.at[a, dp, gx, gy], partner) for a in range(2)]
    arrive(xs[0])

    def project(q, x):
        far = lax.dot_general(W[q, other], x, NT, preferred_element_type=F32)
        for j in range(4):
            SC[q, j] = far[:, 128 * j : 128 * j + 128].astype(BF)
        copy = send(SC.at[q], RC.at[q], core)
        mine = lax.dot_general(W[q, c], x, NT, preferred_element_type=F32)
        for j in range(4):
            PM[q, j] = mine[:, 128 * j : 128 * j + 128]
        return copy

    def chunk(q, k):
        j = lax.rem(zh + k, 4)
        return PM[q, j] + RC[q, j].astype(F32)

    low, high = pl.ds(0, CUT), pl.ds(CUT, HALF - CUT)

    def scatter(q, copy):
        copy.wait_recv()
        SZ[q, 1] = chunk(q, 2).astype(BF)
        first = [
            send(SZ.at[q, 1, low], RA.at[q, low], zdev(2)),
            send(SZ.at[q, 1, high], RA.at[q, high], zdev(-2)),
        ]
        SZ[q, 0, CUT:] = chunk(q, 1)[CUT:].astype(BF)
        SZ[q, 2, :CUT] = chunk(q, 3)[:CUT].astype(BF)
        second = [
            send(SZ.at[q, 0, high], RZ.at[q, 0, high], zdev(2)),
            send(SZ.at[q, 2, low], RZ.at[q, 1, low], zdev(-2)),
        ]
        return first, second

    def relay(q, copies):
        first, second = copies
        first[0].wait_recv()
        SZ[q, 0, :CUT] = (chunk(q, 1)[:CUT] + RA[q, :CUT].astype(F32)).astype(BF)
        second.append(send(SZ.at[q, 0, low], RZ.at[q, 0, low], zdev(2)))
        first[1].wait_recv()
        SZ[q, 2, CUT:] = (chunk(q, 3)[CUT:] + RA[q, CUT:].astype(F32)).astype(BF)
        second.append(send(SZ.at[q, 2, high], RZ.at[q, 1, high], zdev(-2)))

    def total(q, copies):
        arrive(copies[1])
        return chunk(q, 0) + RZ[q, 0].astype(F32) + RZ[q, 1].astype(F32)

    x = T[0, dp].reshape(512, 512)
    gate_c = project(0, x)
    up_c = project(1, x)
    gate_z = scatter(0, gate_c)
    up_z = scatter(1, up_c)
    pass_on(1)
    arrive(swap)
    other_y = [copy for a in range(2) for copy in ysends(a, odp).values()]
    relay(0, gate_z)
    relay(1, up_z)
    arrive(xs[1])
    hg_c = project(2, T[1, dp].reshape(512, 512))
    hg_z = scatter(2, hg_c)
    arrive(other_y)
    other_x = [copy for a in range(2) for copy in xsends(T.at[a, odp, :, gy])]

    right, left, to_core = {}, {}, {}
    near_b = zdev(2 * dp - 1)

    def spread(q, value):
        D[q, dp, c, zh] = value.astype(BF)
        ref = D.at[q, dp, c, zh]
        right[q] = send(ref, ref, zdev(2))
        left[q] = send(ref, ref, zdev(-2))
        to_core[q] = [send(ref, ref, core)]

    def spread_on(q):
        there, back = lax.rem(zh + 3, 4), lax.rem(zh + 1, 4)
        right[q].wait_recv()
        ref = D.at[q, dp, c, there, low]
        right[q] = send(ref, ref, zdev(2))
        ref = D.at[q, dp, c, there]
        to_core[q].append(send(ref, ref, core))
        left[q].wait_recv()
        ref = D.at[q, dp, c, back, high]
        left[q] = send(ref, ref, zdev(-2))
        ref = D.at[q, dp, c, back]
        to_core[q].append(send(ref, ref, core))

    def spread_end(q):
        right[q].wait_recv()
        left[q].wait_recv()
        ref = D.at[q, dp, c, lax.rem(zh + 2, 4)]
        to_core[q].append(send(ref, ref, core))

    def swap_replicas(q):
        refs = [D.at[q, dp, c, lax.rem(zh + 4 + k, 4)] for k in (0, 2 * dp - 1, 1 - 2 * dp)]
        return [
            send(refs[0], refs[0], partner),
            send(refs[0], refs[0], near_b),
            send(refs[1], refs[1], partner),
            send(refs[2], refs[2], near_b),
        ]

    def rows(q, d):
        halves = [
            jnp.concatenate([D[q, d, h, j] for j in range(4)], axis=1) for h in range(2)
        ]
        return jnp.concatenate(halves, axis=0)

    def x_scatter(o, part):
        part = part.astype(BF).reshape(8, 4, 16, 512)
        for g in range(8):
            OB[o, lax.rem(g + 14 - gx, 8)] = part[g]
        groups = []
        for h in range(4):
            block = pl.ds(2 * h, 2)
            groups.append([
                send(OB.at[o, block, lax.rem(gy + k, 4)], RX.at[o, k - 1, block], xdev(k))
                for k in (2, 1, 3)
            ])
        return groups

    def y_scatter(o, h, copies):
        arrive(copies[h])
        block = slice(2 * h, 2 * h + 2)
        value = OB[o, block, gy].astype(F32)
        for k in range(3):
            value = value + RX[o, k, block].astype(F32)
        SY[o, block] = value.astype(BF)
        order = ((1, 0), (2, 3), (4, 5), (7,))[h]
        return [send(SY.at[o, i], RY.at[o, (i + 2) % 8 - 1], ydev((i + 2) % 8)) for i in order]

    def finish(o, copies, ref):
        arrive(copies)
        value = SY[o, 6].astype(F32)
        for k in range(7):
            value = value + RY[o, k].astype(F32)
        FO[o] = value.astype(BF)
        return local(FO.at[o], ref)

    gate_val = total(0, gate_z)
    up_val = total(1, up_z)
    gate_sig = jax.nn.sigmoid(gate_val)
    gate_act = gate_val * gate_sig
    V[0] = up_val * gate_sig * (1.0 + gate_val * (1.0 - gate_sig))
    V[1] = gate_act
    spread(0, gate_act * up_val)
    relay(2, hg_z)
    spread_on(0)
    hid_grad = total(2, hg_z)
    spread(1, hid_grad * V[0])
    spread(2, hid_grad * V[1])
    spread_end(0)
    arrive(to_core[0])
    part = lax.dot_general(rows(0, dp), W[2].reshape(480, 512), TN, preferred_element_type=F32)
    out_x = x_scatter(0, part)
    spread_on(1)
    spread_on(2)
    swapped = [swap_replicas(q) for q in range(3)]
    spread_end(1)
    spread_end(2)
    arrive(to_core[1])
    arrive(to_core[2])
    both = jnp.concatenate([rows(1, dp), rows(2, dp)], axis=0)
    part = lax.dot_general(both, W[0:2].reshape(960, 512), TN, preferred_element_type=F32)
    in_x = x_scatter(1, part)
    out_y = [copy for h in range(4) for copy in y_scatter(0, h, out_x)]

    done = []

    def weight_grad(q, ref):
        right = T[1 if q == 0 else 0].reshape(1024, 512)
        for h in range(2):
            left = jnp.concatenate([D[q, d, h, j] for d in range(2) for j in range(4)], axis=1)
            value = lax.dot_general(left, right, NN, preferred_element_type=F32).astype(BF)
            if h == 0:
                WG[q, 0:HALF] = value
            else:
                WG[q, HALF : HALF + LAST] = value[0:LAST]
        done.append(local(WG.at[q], ref))

    in_y = [copy for h in range(4) for copy in y_scatter(1, h, in_x)]
    late = []
    for q in range(3):
        arrive(swapped[q])
        ref = D.at[q, odp, c]
        late.append(send(ref, ref, core))
    arrive(other_x)
    for q, ref in enumerate((dg_ref, gg_ref, ug_ref)):
        arrive([late[q]])
        weight_grad(q, ref)
    done.append(finish(0, out_y, out_ref))
    done.append(finish(1, in_y, ing_ref))
    for copy in sent:
        copy.wait_send()
    for copy in done:
        copy.wait()


def store(*refs):
    n = (len(refs) - 1) // 3
    sem = refs[-1]
    fetch, put = [], []
    for i in range(n):
        source, result, held = refs[i], refs[n + i], refs[2 * n + i]
        size = source.shape[0]
        cuts = [0, 160, 320, size] if size > 160 else [0, size]
        for start, stop in zip(cuts[:-1], cuts[1:], strict=True):
            rows, k = pl.ds(start, stop - start), len(fetch)
            fetch.append(pltpu.make_async_copy(source.at[rows], held.at[rows], sem.at[0, k]))
            put.append(pltpu.make_async_copy(held.at[rows], result.at[rows], sem.at[1, k]))
    for copy in fetch:
        copy.start()
    for into, out in zip(fetch, put, strict=True):
        into.wait()
        out.start()
    for copy in put:
        copy.wait()


def body(tokens, gate_weight, up_weight, down_weight, out_grad):
    any_spec = pl.BlockSpec(memory_space=pl.ANY)
    hbm_spec = pl.BlockSpec(memory_space=pltpu.HBM)
    small = jax.ShapeDtypeStruct((16, 512), BF)
    large = jax.ShapeDtypeStruct((464, 512), BF)
    results = pl.pallas_call(
        kernel,
        out_shape=(small, small, large, large, large),
        in_specs=[hbm_spec] * 5,
        out_specs=(any_spec,) * 5,
        scratch_shapes=[
            pltpu.VMEM((2, 2, 8, 4, 16, 512), BF),
            pltpu.VMEM((3, 2, HALF, 512), BF),
            pltpu.VMEM((3, 4, HALF, 128), F32),
            pltpu.VMEM((3, 4, HALF, 128), BF),
            pltpu.VMEM((3, 4, HALF, 128), BF),
            pltpu.VMEM((3, 3, HALF, 128), BF),
            pltpu.VMEM((3, HALF, 128), BF),
            pltpu.VMEM((3, 2, HALF, 128), BF),
            pltpu.VMEM((2, HALF, 128), F32),
            pltpu.VMEM((3, 2, 2, 4, HALF, 128), BF),
            pltpu.VMEM((2, 8, 4, 16, 512), BF),
            pltpu.VMEM((2, 3, 8, 16, 512), BF),
            pltpu.VMEM((2, 8, 16, 512), BF),
            pltpu.VMEM((2, 7, 16, 512), BF),
            pltpu.VMEM((3, 464, 512), BF),
            pltpu.VMEM((2, 16, 512), BF),
            pltpu.SemaphoreType.DMA((16,)),
            pltpu.SemaphoreType.DMA((224,)),
            pltpu.SemaphoreType.DMA((224,)),
        ],
        compiler_params=pltpu.CompilerParams(
            collective_id=0, has_side_effects=True, vmem_limit_bytes=62 * 2**20
        ),
        name="block",
    )(tokens, out_grad, gate_weight.T, up_weight.T, down_weight)
    output, input_grad, gate_t, up_t, down_grad = pl.pallas_call(
        store,
        out_shape=(small, small, large, large, large),
        in_specs=[any_spec] * 5,
        out_specs=(hbm_spec,) * 5,
        scratch_shapes=[pltpu.VMEM(r.shape, BF) for r in results] + [pltpu.SemaphoreType.DMA((2, 11))],
        compiler_params=pltpu.CompilerParams(vmem_limit_bytes=62 * 2**20),
        name="store",
    )(*results)
    return output, input_grad, gate_t.T, up_t.T, down_grad


def solution(mesh):
    placed = (
        P(("dp", "gx", "gy"), "gz"),
        P("gz", ("gx", "gy")),
        P("gz", ("gx", "gy")),
        P(("gx", "gy"), "gz"),
        P(("dp", "gx", "gy"), "gz"),
    )
    return jax.shard_map(
        body,
        mesh=mesh,
        in_specs=placed,
        out_specs=(
            P(("dp", "gx", "gy"), "gz"),
            P(("dp", "gx", "gy"), "gz"),
            P("gz", ("gx", "gy")),
            P("gz", ("gx", "gy")),
            P(("gx", "gy"), "gz"),
        ),
        check_vma=False,
    )
```
